512 devices in a mesh: section: 8 (over z_hi, x), feat: 64 (over y, z_lo, core).
Axes of the slice: x: 4, y: 4, z: 16 (z_hi: 2, z_lo: 8; z = z_hi * 8 + z_lo), core: 2. Of those that a mesh axis runs over, the one named last changes fastest.
Arguments:
- pre_tiles: bfloat16 [8, 256, 32, 128], P('section', 'feat'), may hold values from -6 to 6
- block_ids: int32 [8, 256, 32], P('section', 'feat'), may hold values from 0 to 127, all different within a row
- thresholds: float32 [8, 16384], P('section'), may hold values from 0.05 to 1
- decoder: bfloat16 [8, 16384, 2, 2048], P('section', 'feat'), may hold values from -0.09375 to 0.09375
- dec_bias: float32 [8, 2048], P('section'), may hold values from -3 to 3
- targets: bfloat16 [8, 256, 2048], P('section', 'feat'), may hold values from -6 to 6
Outputs:
- grad_tiles: bfloat16 [8, 256, 32, 128], P('section', 'feat')
- grad_decoder: bfloat16 [8, 16384, 2, 2048], P('section', 'feat')
The draws below stay inside these ranges and needn't reach their ends.
Inputs may be any that keep to these rules, and one draw needn't show every extreme that they name: `block_ids`: the 32 block numbers of one token in one layer are distinct.
All inputs are finite; a program needn't handle non-finite values.
Results may differ from the reference program's by a relative error of at most 0.0042.
Values may be sent and summed in bfloat16 or wider, within the bound.
No kernel may reach another device: no remote copies, remote signals or barrier semaphores. Data moves between devices by JAX's collectives and lax.ppermute only.
A program may use at most 64 MiB of HBM per device.

```python
import math
import jax
import jax.numpy as jnp
from jax import lax

D = 2048
F = 16384
BLK = 128
K = 32
R = 2
TOK = 256
L = 8
BLOCKS = 128


def block_levels(stream_key, extent, split, least, top_value):
    factor_of = 1.0
    for axis_at, parts in split:
        steps = jax.random.uniform(jax.random.fold_in(jax.random.fold_in(stream_key, 6), axis_at), (parts,), jnp.float32, least / len(split), top_value / len(split))
        factor_of = factor_of * jnp.repeat(jnp.exp(steps), extent[axis_at] // parts).reshape((-1,) + (1,) * (len(extent) - 1 - axis_at))
    return factor_of


def distinct(key, rows, count, top, lift):
    ranking = jax.random.permutation(jax.random.fold_in(key, 1), count)
    favour = ranking
    for power in range(3):
        favour = favour * favour // count
    favour = favour * lift // count
    lots = jax.random.randint(jax.random.fold_in(key, 2), (rows, count), 0, 4096) + favour
    sure = jax.random.permutation(jax.random.fold_in(key, 3), rows)[jnp.arange(count) % rows]
    lots = jnp.where(jnp.arange(rows)[:, None] == sure[None, :], 1 << 14, lots)
    merit = lots * count + jnp.arange(count)
    return lax.top_k(merit.astype(jnp.int32), top)[1].astype(jnp.int32)


def noise(stream_key, dims, deviation, limit, split=(), held_as=jnp.bfloat16):
    array = deviation * jax.random.normal(stream_key, dims, jnp.float32)
    if split:
        array = array * block_levels(stream_key, dims, split, -0.22, 0.18)
    return jnp.clip(array, -limit, limit).astype(held_as)


def setup_inputs(seed: int = 0) -> dict:
    seeds = jax.random.split(jax.random.key(seed), 7)
    return {
        "pre_tiles": noise(seeds[0], (L, TOK, K, BLK), 1.0, 6.0, ((0, 8), (1, 64))),
        "block_ids": distinct(seeds[1], L * TOK, BLOCKS, K, 2048).reshape((L, TOK, K)),
        "thresholds": jnp.clip(jnp.exp(math.log(1.0) - 2.9957323 * jax.random.uniform(seeds[2], (L, F), jnp.float32) ** block_levels(seeds[2], (L, F), ((0, 8),), -0.2, 0.2)), 0.05, 1.0),
        "decoder": noise(seeds[3], (L, F, R, D), (K * BLK) ** -0.5, 0.09375, ((0, 8), (1, 64))),
        "dec_bias": noise(seeds[4], (L, D), 0.5, 3.0, ((0, 8),), jnp.float32),
        "targets": noise(seeds[5], (L, TOK, D), 1.0, 6.0, ((0, 8), (1, 64))),
    }


def tile_columns(block_list):
    offsets = jnp.arange(BLK, dtype=jnp.int32)
    return block_list[:, :, None] * BLK + offsets[None, None, :]


def tile_rows(block_list):
    tok_count = block_list.shape[0]
    return jnp.broadcast_to(jnp.arange(tok_count, dtype=jnp.int32)[:, None, None], (tok_count, block_list.shape[1], BLK))


def reference(pre_tiles, block_ids, thresholds, decoder, dec_bias, targets):
    partials = []
    feature_list = []
    for layer in range(L):
        columns = tile_columns(block_ids[layer])
        row_index = tile_rows(block_ids[layer])
        dense = jnp.zeros((TOK, F), pre_tiles.dtype).at[row_index, columns].add(pre_tiles[layer])
        features = jnp.where(dense > thresholds[layer][None, :], dense, jnp.zeros_like(dense))
        weights = decoder[layer].reshape(F, R * D)
        partials.append(jnp.dot(features, weights, preferred_element_type=jnp.float32))
        feature_list.append(features)
    error_list = []
    for layer in range(L):
        recon = partials[layer][:, :D] + dec_bias[layer][None, :]
        if layer > 0:
            recon = recon + partials[layer - 1][:, D:]
        error_list.append((recon - targets[layer].astype(jnp.float32)).astype(jnp.bfloat16))
    zero_rows = jnp.zeros_like(error_list[0])
    tile_grads = []
    dec_grads = []
    for layer in range(L):
        following = error_list[layer + 1] if layer + 1 < L else zero_rows
        extended = jnp.concatenate([error_list[layer], following], axis=1)
        weights = decoder[layer].reshape(F, R * D)
        feature_grad = jnp.dot(extended, weights.T, preferred_element_type=jnp.float32).astype(jnp.bfloat16)
        columns = tile_columns(block_ids[layer])
        row_index = tile_rows(block_ids[layer])
        picked = feature_grad[row_index, columns]
        gate_open = pre_tiles[layer] > thresholds[layer][columns]
        tile_grads.append(jnp.where(gate_open, picked, jnp.zeros_like(picked)))
        grad_dec = jnp.dot(feature_list[layer].T, extended, preferred_element_type=jnp.float32)
        dec_grads.append(grad_dec.astype(jnp.bfloat16).reshape(F, R, D))
    return jnp.stack(tile_grads), jnp.stack(dec_grads)
```

```python
import jax
import jax.numpy as jnp
from jax import lax
from jax.sharding import Mesh, PartitionSpec as P

BLK = 128
AXES = ("zh", "x", "y", "z", "c")
SIZES = (2, 4, 4, 8, 2)
SECTION, FEAT, CHIP = ("zh", "x"), ("y", "z", "c"), ("y", "z")
WIRE = jnp.float32


def swap_cores(block):
    return lax.ppermute(block, "c", [(0, 1), (1, 0)])


def exchange(block, axis):
    return lax.all_to_all(block, axis, split_axis=0, concat_axis=0, tiled=True)


def gather_rows(block, axis):
    copies = jnp.broadcast_to(block[None], (lax.axis_size(axis),) + block.shape)
    got = exchange(copies, axis)
    return got.reshape((-1,) + block.shape[1:])


def section_swap(block):
    route = []
    layers = SIZES[0] * SIZES[1]
    for layer in range(layers - 1):
        route.append((2 * layer + 1, 2 * layer + 2))
        route.append((2 * layer + 2, 2 * layer + 1))
    return lax.ppermute(block, ("zh", "x", "c"), route)


def per_device(pre_tiles, block_ids, thresholds, decoder, dec_bias, targets):
    bf16, f32 = jnp.bfloat16, jnp.float32
    core = lax.axis_index("c")
    layer = lax.axis_index(SECTION)
    last_layer = SIZES[0] * SIZES[1] - 1
    chips = SIZES[2] * SIZES[3]
    tiles, ids = pre_tiles[0], block_ids[0]
    tok_local = tiles.shape[0]
    blocks = thresholds.shape[1] // BLK
    feat_dev = decoder.shape[1]
    width = decoder.shape[3]

    weights = decoder[0]
    w_mine = lax.dynamic_index_in_dim(weights, core, 1, keepdims=False)
    w_other = lax.dynamic_index_in_dim(weights, 1 - core, 1, keepdims=False)
    w_partner = swap_cores(w_other)
    partner_targets = swap_cores(targets[0])

    selector = (ids[:, :, None] == jnp.arange(blocks, dtype=jnp.int32)[None, None, :]).astype(bf16)
    dense = jnp.einsum("tkb,tkc->tbc", selector, tiles, preferred_element_type=f32)
    floor = thresholds[0].reshape(blocks, BLK)
    own_rows = jnp.where(dense > floor[None], dense, 0.0).astype(bf16)
    own_rows = own_rows.reshape(tok_local, chips, 2 * feat_dev).transpose(1, 0, 2)
    half = exchange(own_rows, CHIP)
    other_half = swap_cores(half)
    first = jnp.where(core == 0, half, other_half)
    second = jnp.where(core == 0, other_half, half)
    features = jnp.concatenate([first, second], axis=1).reshape(-1, 2 * feat_dev)
    tokens = features.shape[0]
    f_mine = lax.dynamic_slice_in_dim(features, core * feat_dev, feat_dev, 1)
    f_other = lax.dynamic_slice_in_dim(features, (1 - core) * feat_dev, feat_dev, 1)

    part = jnp.dot(f_mine, w_mine, preferred_element_type=f32)
    part = part + jnp.dot(f_other, w_partner, preferred_element_type=f32)
    part = part.astype(WIRE).reshape(SIZES[2], tokens // SIZES[2], width)
    part = jnp.sum(exchange(part, "y").astype(f32), axis=0)
    part = part.astype(WIRE).reshape(SIZES[3], -1, width)
    part = jnp.sum(exchange(part, "z").astype(f32), axis=0)

    rows = jnp.concatenate([targets[0], partner_targets], axis=0).astype(f32)
    shift = jnp.where(core == 0, dec_bias[0][None, :] - rows, 0.0)
    mine = part + shift
    error = mine + section_swap(mine)
    error = jnp.where((core == 1) & (layer == last_layer), 0.0, error).astype(bf16)

    e_mine = gather_rows(gather_rows(error, "z"), "y")
    e_other = swap_cores(e_mine)

    contract = (((1,), (1,)), ((), ()))
    grad = lax.dot_general(e_mine, w_mine, contract, preferred_element_type=f32)
    grad = grad + lax.dot_general(e_other, w_other, contract, preferred_element_type=f32)
    grad = jnp.where(f_mine > 0, grad, 0.0).astype(bf16)
    returned = exchange(grad.reshape(2 * chips, tok_local, feat_dev), FEAT)

    e_first = jnp.where(core == 0, e_mine, e_other)
    e_second = jnp.where(core == 0, e_other, e_mine)
    extended = jnp.concatenate([e_first, e_second], axis=1)
    dec = lax.dot_general(f_mine, extended, (((0,), (0,)), ((), ())), preferred_element_type=f32)
    grad_decoder = dec.astype(bf16).reshape(1, feat_dev, 2, width)

    table = returned.transpose(1, 0, 2).reshape(tok_local, blocks, BLK)
    picked = jnp.einsum("tkb,tbc->tkc", selector, table, preferred_element_type=f32)
    return picked.astype(bf16)[None], grad_decoder


def solution(mesh):
    split = Mesh(mesh.devices.reshape(SIZES), AXES)
    placed = (
        P(SECTION, FEAT, None, None),
        P(SECTION, FEAT, None),
        P(SECTION, None),
        P(SECTION, FEAT, None, None),
        P(SECTION, None),
        P(SECTION, FEAT, None),
    )
    return jax.shard_map(
        per_device,
        mesh=split,
        in_specs=placed,
        out_specs=(P(SECTION, FEAT, None, None), P(SECTION, FEAT, None, None)),
        check_vma=False,
    )
```

```python
import functools

import jax
import jax.numpy as jnp
from jax import lax
from jax.experimental import pallas as pl
from jax.experimental.pallas import tpu as pltpu
from jax.sharding import Mesh, PartitionSpec as P

BLK = 128
AXES = ("zh", "x", "y", "z", "c")
SIZES = (2, 4, 4, 8, 2)
SECTION, FEAT = ("zh", "x"), ("y", "z", "c")
WIRE_Y = jnp.float32
WIRE_Z = jnp.float32


def swap_cores(block):
    return lax.ppermute(block, "c", [(0, 1), (1, 0)])


def exchange(block, axis):
    return lax.all_to_all(block, axis, split_axis=0, concat_axis=0, tiled=True)


def gather(block, axis):
    copies = jnp.broadcast_to(block[None], (lax.axis_size(axis),) + block.shape)
    return exchange(copies, axis)


def to_layer(block, distance):
    layers = SIZES[0] * SIZES[1]
    route = [(i, i + distance) for i in range(layers) if 0 <= i + distance < layers]
    return lax.ppermute(block, SECTION, route)


def column_blocks(error_ref, col):
    for z in range(error_ref.shape[1]):
        for r in range(error_ref.shape[3] // col):
            block = error_ref[:, z, :, r * col : (r + 1) * col]
            yield z, r, block.reshape(-1, col)


def grad_kernel(col, error_ref, *refs):
    *weight_refs, grad_ref, total = refs
    step = pl.program_id(0)
    feat_dev = weight_refs[0].shape[0]

    @pl.when(step == 0)
    def _():
        total[...] = jnp.zeros_like(total)

    for z, r, block in column_blocks(error_ref, col):
        for half in range(2):
            weight = weight_refs[2 * half + r][:, z * col : (z + 1) * col]
            total[:, half * feat_dev : (half + 1) * feat_dev] += lax.dot_general(
                block, weight, (((1,), (1,)), ((), ())), preferred_element_type=jnp.float32
            )

    @pl.when(step == pl.num_programs(0) - 1)
    def _():
        grad_ref[...] = total[...].astype(grad_ref.dtype)


def feature_grads(error, weights, weights_other):
    ny, nz, rows, both = error.shape
    feat_dev = weights.shape[0]
    steps = 4
    wide = weights.shape[1] // 2 // steps
    blocks = [
        pl.BlockSpec((feat_dev, wide), lambda j, r=r: (0, r * steps + j)) for r in range(2)
    ]
    return pl.pallas_call(
        functools.partial(grad_kernel, both // 2),
        grid=(steps,),
        in_specs=[pl.BlockSpec((ny, nz // steps, rows, both), lambda j: (0, j, 0, 0))] + 2 * blocks,
        out_specs=pl.BlockSpec((ny * rows, 2 * feat_dev), lambda j: (0, 0)),
        out_shape=jax.ShapeDtypeStruct((ny * rows, 2 * feat_dev), error.dtype),
        scratch_shapes=[pltpu.VMEM((ny * rows, 2 * feat_dev), jnp.float32)],
        compiler_params=pltpu.CompilerParams(vmem_limit_bytes=24 << 20),
        cost_estimate=pl.CostEstimate(
            flops=2 * error.size * 2 * feat_dev, bytes_accessed=5 << 20, transcendentals=0
        ),
    )(error, weights, weights, weights_other, weights_other)


def decoder_kernel(col, feature_ref, error_ref, other_ref, out_ref):
    half = feature_ref.shape[1] // 2
    for (z, r, block), (_, _, other) in zip(
        column_blocks(error_ref, col), column_blocks(other_ref, col)
    ):
        total = jnp.dot(feature_ref[:, :half], block, preferred_element_type=jnp.float32)
        total += jnp.dot(feature_ref[:, half:], other, preferred_element_type=jnp.float32)
        out_ref[r, :, z * col : (z + 1) * col] = total.astype(out_ref.dtype)


def decoder_grads(features, error, error_other):
    ny, nz, rows, both = error.shape
    feat_dev = features.shape[0]
    steps = 4
    block = pl.BlockSpec((ny, nz // steps, rows, both), lambda j: (0, j, 0, 0))
    width = nz * both // 2
    return pl.pallas_call(
        functools.partial(decoder_kernel, both // 2),
        grid=(steps,),
        in_specs=[pl.BlockSpec(features.shape, lambda j: (0, 0)), block, block],
        out_specs=pl.BlockSpec((2, feat_dev, width // steps), lambda j: (0, 0, j)),
        out_shape=jax.ShapeDtypeStruct((2, feat_dev, width), error.dtype),
        compiler_params=pltpu.CompilerParams(vmem_limit_bytes=24 << 20),
        cost_estimate=pl.CostEstimate(
            flops=4 * error.size * feat_dev, bytes_accessed=4 << 20, transcendentals=0
        ),
    )(features, error, error_other)


def per_device(pre_tiles, block_ids, thresholds, decoder, dec_bias, targets):
    bf16, f32 = jnp.bfloat16, jnp.float32
    ny, nz, nc = SIZES[2:]
    core = lax.axis_index("c")
    chip = lax.axis_index(("y", "z"))
    layer = lax.axis_index(SECTION)
    last_layer = SIZES[0] * SIZES[1] - 1
    tiles, ids = pre_tiles[0], block_ids[0]
    tok = tiles.shape[0]
    blocks = thresholds.shape[1] // BLK
    feat_dev = decoder.shape[1]
    width = decoder.shape[3]
    own_blocks = feat_dev // BLK
    col = width // nz

    order = jnp.arange(blocks, dtype=jnp.int32) ^ (core * own_blocks)
    selector = (ids[:, :, None] == order[None, None, :]).astype(bf16)
    dense = jnp.einsum("tkb,tkc->tbc", selector, tiles, preferred_element_type=f32)
    floor = thresholds[0].reshape(-1, nc, own_blocks, BLK)
    floor = jnp.where(core == 0, floor, floor[:, ::-1]).reshape(blocks, BLK)
    own = jnp.where(dense > floor[None], dense, 0.0).astype(bf16)
    sent = own.reshape(tok, ny * nz, nc * feat_dev).transpose(1, 0, 2)
    features = exchange(sent, ("y", "z")).reshape(ny * nz * tok, nc * feat_dev)
    f_mine, f_other = features[:, :feat_dev], features[:, feat_dev:]

    weights = lax.optimization_barrier(decoder[0].reshape(feat_dev, nc * width))
    weights_other = swap_cores(weights)

    part = jnp.dot(f_mine, weights, preferred_element_type=f32)
    part = part + jnp.dot(f_other, weights_other, preferred_element_type=f32)
    shift = dec_bias[0][None, :] - targets[0].astype(f32)
    shift = jnp.concatenate([shift, jnp.zeros_like(shift)], axis=1)
    here = jnp.arange(ny * nz)[:, None, None] == chip
    part = part + jnp.where(here, shift[None], 0.0).reshape(part.shape)
    part = part.astype(WIRE_Y).reshape(ny, nz * tok, nc * width)
    part = jnp.sum(exchange(part, "y").astype(f32), axis=0)
    part = part.reshape(nz * tok, nc, nz, col).transpose(2, 0, 1, 3).astype(WIRE_Z)
    part = jnp.sum(exchange(part.reshape(nz, nz * tok, nc * col), "z").astype(f32), axis=0)

    mine, beyond = part[:, :col], part[:, col:]
    got, got_next = lax.optimization_barrier((to_layer(beyond, 1), to_layer(mine, -1)))
    error_next = jnp.where(layer == last_layer, 0.0, beyond + got_next)
    error = jnp.concatenate([mine + got, error_next], axis=1).astype(bf16)

    error = gather(gather(error, "z"), "y").reshape(ny, nz, nz * tok, nc * col)
    error_other = swap_cores(error)

    grad = feature_grads(error, weights, weights_other).reshape(ny * nz, tok, -1)
    grad, error_other = lax.optimization_barrier((grad, error_other))
    returned = exchange(grad, ("y", "z"))

    f_own = jnp.concatenate([f_mine, swap_cores(f_other)], axis=0).T
    grad_decoder = decoder_grads(f_own, error, error_other).transpose(1, 0, 2)[None]

    table = returned.transpose(1, 0, 2).reshape(tok, blocks, BLK)
    table = jnp.where(own > 0, table, jnp.zeros_like(table))
    picked = jnp.einsum("tkb,tbc->tkc", selector, table, preferred_element_type=f32)
    return picked.astype(bf16)[None], grad_decoder


def solution(mesh):
    split = Mesh(mesh.devices.reshape(SIZES), AXES)
    placed = (
        P(SECTION, FEAT, None, None),
        P(SECTION, FEAT, None),
        P(SECTION, None),
        P(SECTION, FEAT, None, None),
        P(SECTION, None),
        P(SECTION, FEAT, None),
    )
    return jax.shard_map(
        per_device,
        mesh=split,
        in_specs=placed,
        out_specs=(P(SECTION, FEAT, None, None), P(SECTION, FEAT, None, None)),
        check_vma=False,
    )
```

```python
import functools

import jax
import jax.numpy as jnp
from jax import lax
from jax.experimental import pallas as pl
from jax.experimental.pallas import tpu as pltpu
from jax.sharding import Mesh, PartitionSpec as P

BLK = 128
AXES = ("zh", "x", "y", "z", "c")
SIZES = (2, 4, 4, 8, 2)
SECTION, FEAT = ("zh", "x"), ("y", "z", "c")
WIRE_Y = jnp.bfloat16
WIRE_Z = jnp.bfloat16


def swap_cores(block):
    return lax.ppermute(block, "c", [(0, 1), (1, 0)])


def exchange(block, axis):
    return lax.all_to_all(block, axis, split_axis=0, concat_axis=0, tiled=True)


def gather(block, axis):
    copies = jnp.broadcast_to(block[None], (lax.axis_size(axis),) + block.shape)
    return exchange(copies, axis)


def with_neighbours(mine, beyond):
    layers = SIZES[0] * SIZES[1]
    even = lax.axis_index(SECTION) % 2 == 0
    rounds = []
    for first, sent in ((0, jnp.where(even, beyond, mine)), (1, jnp.where(even, mine, beyond))):
        route = []
        for i in range(first, layers - 1, 2):
            route += [(i, i + 1), (i + 1, i)]
        rounds.append(lax.ppermute(sent, SECTION, route))
    lower, upper = lax.optimization_barrier(tuple(rounds))
    return jnp.where(even, upper, lower), jnp.where(even, lower, upper)


def column_blocks(error_ref, col):
    for z in range(error_ref.shape[1]):
        for r in range(error_ref.shape[3] // col):
            block = error_ref[:, z, :, r * col : (r + 1) * col]
            yield z, r, block.reshape(-1, col)


def grad_kernel(col, error_ref, *refs):
    *weight_refs, grad_ref, total = refs
    step = pl.program_id(0)
    feat_dev = weight_refs[0].shape[0]

    @pl.when(step == 0)
    def _():
        total[...] = jnp.zeros_like(total)

    for z, r, block in column_blocks(error_ref, col):
        for half in range(2):
            weight = weight_refs[2 * half + r][:, z * col : (z + 1) * col]
            total[:, half * feat_dev : (half + 1) * feat_dev] += lax.dot_general(
                block, weight, (((1,), (1,)), ((), ())), preferred_element_type=jnp.float32
            )

    @pl.when(step == pl.num_programs(0) - 1)
    def _():
        grad_ref[...] = total[...].astype(grad_ref.dtype)


def feature_grads(error, weights, weights_other):
    ny, nz, rows, both = error.shape
    feat_dev = weights.shape[0]
    steps = 4
    wide = weights.shape[1] // 2 // steps
    blocks = [
        pl.BlockSpec((feat_dev, wide), lambda j, r=r: (0, r * steps + j)) for r in range(2)
    ]
    return pl.pallas_call(
        functools.partial(grad_kernel, both // 2),
        grid=(steps,),
        in_specs=[pl.BlockSpec((ny, nz // steps, rows, both), lambda j: (0, j, 0, 0))] + 2 * blocks,
        out_specs=pl.BlockSpec((ny * rows, 2 * feat_dev), lambda j: (0, 0)),
        out_shape=jax.ShapeDtypeStruct((ny * rows, 2 * feat_dev), error.dtype),
        scratch_shapes=[pltpu.VMEM((ny * rows, 2 * feat_dev), jnp.float32)],
        compiler_params=pltpu.CompilerParams(vmem_limit_bytes=24 << 20),
        cost_estimate=pl.CostEstimate(
            flops=2 * error.size * 2 * feat_dev, bytes_accessed=5 << 20, transcendentals=0
        ),
    )(error, weights, weights, weights_other, weights_other)


def decoder_kernel(col, feature_ref, error_ref, other_ref, out_ref):
    half = feature_ref.shape[1] // 2
    for (z, r, block), (_, _, other) in zip(
        column_blocks(error_ref, col), column_blocks(other_ref, col)
    ):
        total = jnp.dot(feature_ref[:, :half], block, preferred_element_type=jnp.float32)
        total += jnp.dot(feature_ref[:, half:], other, preferred_element_type=jnp.float32)
        out_ref[r, :, z * col : (z + 1) * col] = total.astype(out_ref.dtype)


def decoder_grads(features, error, error_other):
    ny, nz, rows, both = error.shape
    feat_dev = features.shape[0]
    steps = 4
    block = pl.BlockSpec((ny, nz // steps, rows, both), lambda j: (0, j, 0, 0))
    width = nz * both // 2
    return pl.pallas_call(
        functools.partial(decoder_kernel, both // 2),
        grid=(steps,),
        in_specs=[pl.BlockSpec(features.shape, lambda j: (0, 0)), block, block],
        out_specs=pl.BlockSpec((2, feat_dev, width // steps), lambda j: (0, 0, j)),
        out_shape=jax.ShapeDtypeStruct((2, feat_dev, width), error.dtype),
        compiler_params=pltpu.CompilerParams(vmem_limit_bytes=24 << 20),
        cost_estimate=pl.CostEstimate(
            flops=4 * error.size * feat_dev, bytes_accessed=4 << 20, transcendentals=0
        ),
    )(features, error, error_other)


def per_device(pre_tiles, block_ids, thresholds, decoder, dec_bias, targets):
    bf16, f32 = jnp.bfloat16, jnp.float32
    ny, nz, nc = SIZES[2:]
    core = lax.axis_index("c")
    chip = lax.axis_index(("y", "z"))
    layer = lax.axis_index(SECTION)
    last_layer = SIZES[0] * SIZES[1] - 1
    tiles, ids = pre_tiles[0], block_ids[0]
    tok = tiles.shape[0]
    blocks = thresholds.shape[1] // BLK
    feat_dev = decoder.shape[1]
    width = decoder.shape[3]
    own_blocks = feat_dev // BLK
    col = width // nz

    order = jnp.arange(blocks, dtype=jnp.int32) ^ (core * own_blocks)
    selector = (ids[:, :, None] == order[None, None, :]).astype(bf16)
    dense = jnp.einsum("tkb,tkc->tbc", selector, tiles, preferred_element_type=f32)
    floor = thresholds[0].reshape(-1, nc, own_blocks, BLK)
    floor = jnp.where(core == 0, floor, floor[:, ::-1]).reshape(blocks, BLK)
    own = jnp.where(dense > floor[None], dense, 0.0).astype(bf16)
    sent = own.reshape(tok, ny * nz, nc * feat_dev).transpose(1, 0, 2)
    features = exchange(sent, ("y", "z")).reshape(ny * nz * tok, nc * feat_dev)
    f_mine, f_other = features[:, :feat_dev], features[:, feat_dev:]

    weights = lax.optimization_barrier(decoder[0].reshape(feat_dev, nc * width))
    weights_other = swap_cores(weights)

    part = jnp.dot(f_mine, weights, preferred_element_type=f32)
    part = part + jnp.dot(f_other, weights_other, preferred_element_type=f32)
    shift = dec_bias[0][None, :] - targets[0].astype(f32)
    shift = jnp.concatenate([shift, jnp.zeros_like(shift)], axis=1)
    here = jnp.arange(ny * nz)[:, None, None] == chip
    part = part + jnp.where(here, shift[None], 0.0).reshape(part.shape)
    part = part.astype(WIRE_Y).reshape(ny, nz * tok, nc * width)
    part = jnp.sum(exchange(part, "y").astype(f32), axis=0)
    f_swapped = swap_cores(f_other)
    part, f_swapped = lax.optimization_barrier((part, f_swapped))
    part = part.reshape(nz * tok, nc, nz, col).transpose(2, 0, 1, 3).astype(WIRE_Z)
    part = jnp.sum(exchange(part.reshape(nz, nz * tok, nc * col), "z").astype(f32), axis=0)

    mine, beyond = part[:, :col], part[:, col:]
    got, got_next = with_neighbours(mine, beyond)
    error_next = jnp.where(layer == last_layer, 0.0, beyond + got_next)
    error = jnp.concatenate([mine + got, error_next], axis=1).astype(bf16)

    error = gather(gather(error, "z"), "y").reshape(ny, nz, nz * tok, nc * col)
    error_other = swap_cores(error)

    grad = feature_grads(error, weights, weights_other).reshape(ny * nz, tok, -1)
    grad, error_other = lax.optimization_barrier((grad, error_other))
    returned = exchange(grad, ("y", "z"))

    f_own = jnp.concatenate([f_mine, f_swapped], axis=0).T
    grad_decoder = decoder_grads(f_own, error, error_other).transpose(1, 0, 2)[None]

    table = returned.transpose(1, 0, 2).reshape(tok, blocks, BLK)
    table = jnp.where(own > 0, table, jnp.zeros_like(table))
    picked = jnp.einsum("tkb,tbc->tkc", selector, table, preferred_element_type=f32)
    return picked.astype(bf16)[None], grad_decoder


def solution(mesh):
    split = Mesh(mesh.devices.reshape(SIZES), AXES)
    placed = (
        P(SECTION, FEAT, None, None),
        P(SECTION, FEAT, None),
        P(SECTION, None),
        P(SECTION, FEAT, None, None),
        P(SECTION, None),
        P(SECTION, FEAT, None),
    )
    return jax.shard_map(
        per_device,
        mesh=split,
        in_specs=placed,
        out_specs=(P(SECTION, FEAT, None, None), P(SECTION, FEAT, None, None)),
        check_vma=False,
    )
```

```python
import functools

import jax
import jax.numpy as jnp
from jax import lax
from jax.experimental import pallas as pl
from jax.experimental.pallas import tpu as pltpu
from jax.sharding import Mesh, PartitionSpec as P

BLK = 128
AXES = ("zh", "x", "y", "z", "c")
SIZES = (2, 4, 4, 8, 2)
SECTION, FEAT = ("zh", "x"), ("y", "z", "c")
WIRE_Y = jnp.bfloat16
WIRE_Z = jnp.bfloat16


def swap_cores(block):
    return lax.ppermute(block, "c", [(0, 1), (1, 0)])


def exchange(block, axis):
    return lax.all_to_all(block, axis, split_axis=0, concat_axis=0, tiled=True)


def gather(block, axis):
    copies = jnp.broadcast_to(block[None], (lax.axis_size(axis),) + block.shape)
    return exchange(copies, axis)


def with_neighbours(mine, beyond):
    layers, nz = SIZES[0] * SIZES[1], SIZES[3]
    even = lax.axis_index(SECTION) % 2 == 0
    rounds = []
    for first, sent in ((0, jnp.where(even, beyond, mine)), (1, jnp.where(even, mine, beyond))):
        route = []
        for i in range(first, layers - 1, 2):
            far = (i + 1) % SIZES[1] == 0
            for z in range(nz):
                here, there = i * nz + z, (i + 1) * nz + (nz - 1 - z if far else z)
                route += [(here, there), (there, here)]
        rounds.append(lax.ppermute(sent, SECTION + ("z",), route))
    lower, upper = lax.optimization_barrier(tuple(rounds))
    return jnp.where(even, upper, lower), jnp.where(even, lower, upper)


def column_blocks(error_ref, col):
    for z in range(error_ref.shape[1]):
        for r in range(error_ref.shape[3] // col):
            block = error_ref[:, z, :, r * col : (r + 1) * col]
            yield z, r, block.reshape(-1, col)


def grad_kernel(col, error_ref, *refs):
    *weight_refs, grad_ref, total = refs
    step = pl.program_id(0)
    feat_dev = weight_refs[0].shape[0]

    @pl.when(step == 0)
    def _():
        total[...] = jnp.zeros_like(total)

    for z, r, block in column_blocks(error_ref, col):
        for half in range(2):
            weight = weight_refs[2 * half + r][:, z * col : (z + 1) * col]
            total[:, half * feat_dev : (half + 1) * feat_dev] += lax.dot_general(
                block, weight, (((1,), (1,)), ((), ())), preferred_element_type=jnp.float32
            )

    @pl.when(step == pl.num_programs(0) - 1)
    def _():
        grad_ref[...] = total[...].astype(grad_ref.dtype)


def feature_grads(error, weights, weights_other):
    ny, nz, rows, both = error.shape
    feat_dev = weights.shape[0]
    steps = 4
    wide = weights.shape[1] // 2 // steps
    blocks = [
        pl.BlockSpec((feat_dev, wide), lambda j, r=r: (0, r * steps + j)) for r in range(2)
    ]
    return pl.pallas_call(
        functools.partial(grad_kernel, both // 2),
        grid=(steps,),
        in_specs=[pl.BlockSpec((ny, nz // steps, rows, both), lambda j: (0, j, 0, 0))] + 2 * blocks,
        out_specs=pl.BlockSpec((ny * rows, 2 * feat_dev), lambda j: (0, 0)),
        out_shape=jax.ShapeDtypeStruct((ny * rows, 2 * feat_dev), error.dtype),
        scratch_shapes=[pltpu.VMEM((ny * rows, 2 * feat_dev), jnp.float32)],
        compiler_params=pltpu.CompilerParams(vmem_limit_bytes=24 << 20),
        cost_estimate=pl.CostEstimate(
            flops=2 * error.size * 2 * feat_dev, bytes_accessed=5 << 20, transcendentals=0
        ),
    )(error, weights, weights, weights_other, weights_other)


def decoder_kernel(col, feature_ref, error_ref, other_ref, out_ref):
    half = feature_ref.shape[1] // 2
    for (z, r, block), (_, _, other) in zip(
        column_blocks(error_ref, col), column_blocks(other_ref, col)
    ):
        total = jnp.dot(feature_ref[:, :half], block, preferred_element_type=jnp.float32)
        total += jnp.dot(feature_ref[:, half:], other, preferred_element_type=jnp.float32)
        out_ref[r, :, z * col : (z + 1) * col] = total.astype(out_ref.dtype)


def decoder_grads(features, error, error_other):
    ny, nz, rows, both = error.shape
    feat_dev = features.shape[0]
    steps = 4
    block = pl.BlockSpec((ny, nz // steps, rows, both), lambda j: (0, j, 0, 0))
    width = nz * both // 2
    return pl.pallas_call(
        functools.partial(decoder_kernel, both // 2),
        grid=(steps,),
        in_specs=[pl.BlockSpec(features.shape, lambda j: (0, 0)), block, block],
        out_specs=pl.BlockSpec((2, feat_dev, width // steps), lambda j: (0, 0, j)),
        out_shape=jax.ShapeDtypeStruct((2, feat_dev, width), error.dtype),
        compiler_params=pltpu.CompilerParams(vmem_limit_bytes=24 << 20),
        cost_estimate=pl.CostEstimate(
            flops=4 * error.size * feat_dev, bytes_accessed=4 << 20, transcendentals=0
        ),
    )(features, error, error_other)


def per_device(pre_tiles, block_ids, thresholds, decoder, dec_bias, targets):
    bf16, f32 = jnp.bfloat16, jnp.float32
    ny, nz, nc = SIZES[2:]
    core = lax.axis_index("c")
    layer = lax.axis_index(SECTION)
    last_layer = SIZES[0] * SIZES[1] - 1
    tiles, ids = pre_tiles[0], block_ids[0]
    tok = tiles.shape[0]
    blocks = thresholds.shape[1] // BLK
    feat_dev = decoder.shape[1]
    width = decoder.shape[3]
    own_blocks = feat_dev // BLK
    col = width // nz

    order = jnp.arange(blocks, dtype=jnp.int32) ^ (core * own_blocks)
    selector = (ids[:, :, None] == order[None, None, :]).astype(bf16)
    dense = jnp.einsum("tkb,tkc->tbc", selector, tiles, preferred_element_type=f32)
    floor = thresholds[0].reshape(-1, nc, own_blocks, BLK)
    floor = jnp.where(core == 0, floor, floor[:, ::-1]).reshape(blocks, BLK)
    own = jnp.where(dense > floor[None], dense, 0.0).astype(bf16)
    sent = own.reshape(tok, ny * nz, nc * feat_dev).transpose(1, 0, 2)
    features = exchange(sent, ("y", "z")).reshape(ny * nz * tok, nc * feat_dev)
    f_mine, f_other = features[:, :feat_dev], features[:, feat_dev:]

    weights = lax.optimization_barrier(decoder[0].reshape(feat_dev, nc * width))
    weights_other = swap_cores(weights)

    part = jnp.dot(f_mine, weights, preferred_element_type=f32)
    part = part + jnp.dot(f_other, weights_other, preferred_element_type=f32)
    part = part.astype(WIRE_Y).reshape(ny, nz * tok, nc * width)
    part = jnp.sum(exchange(part, "y").astype(f32), axis=0)
    shift = dec_bias[0][None, :] - targets[0].astype(f32)
    shift = jnp.concatenate([shift, jnp.zeros_like(shift)], axis=1)
    here = jnp.arange(nz)[:, None, None] == lax.axis_index("z")
    part = part + jnp.where(here, shift[None], 0.0).reshape(part.shape)
    f_swapped = swap_cores(f_other)
    part, f_swapped = lax.optimization_barrier((part, f_swapped))
    mirrored = lax.axis_index("zh") % 2 == 1
    part = part.reshape(nz * tok, nc, nz, col).transpose(2, 0, 1, 3).astype(WIRE_Z)
    part = part.reshape(nz, nz * tok, nc * col)
    part = jnp.where(mirrored, part[::-1], part)
    part = jnp.sum(exchange(part, "z").astype(f32), axis=0)

    mine, beyond = part[:, :col], part[:, col:]
    got, got_next = with_neighbours(mine, beyond)
    error_next = jnp.where(layer == last_layer, 0.0, beyond + got_next)
    error = jnp.concatenate([mine + got, error_next], axis=1).astype(bf16)

    error = gather(error, "z").reshape(nz, nz * tok, nc * col)
    error = jnp.where(mirrored, error[::-1], error)
    error = gather(error, "y")
    error_other = swap_cores(error)

    grad = feature_grads(error, weights, weights_other).reshape(ny * nz, tok, -1)
    grad, error_other = lax.optimization_barrier((grad, error_other))
    returned = exchange(grad, ("y", "z"))

    f_own = jnp.concatenate([f_mine, f_swapped], axis=0).T
    grad_decoder = decoder_grads(f_own, error, error_other).transpose(1, 0, 2)[None]

    table = returned.transpose(1, 0, 2).reshape(tok, blocks, BLK)
    table = jnp.where(own > 0, table, jnp.zeros_like(table))
    picked = jnp.einsum("tkb,tbc->tkc", selector, table, preferred_element_type=f32)
    return picked.astype(bf16)[None], grad_decoder


def solution(mesh):
    split = Mesh(mesh.devices.reshape(SIZES), AXES)
    placed = (
        P(SECTION, FEAT, None, None),
        P(SECTION, FEAT, None),
        P(SECTION, None),
        P(SECTION, FEAT, None, None),
        P(SECTION, None),
        P(SECTION, FEAT, None),
    )
    return jax.shard_map(
        per_device,
        mesh=split,
        in_specs=placed,
        out_specs=(P(SECTION, FEAT, None, None), P(SECTION, FEAT, None, None)),
        check_vma=False,
    )
```

```python
import functools

import jax
import jax.numpy as jnp
from jax import lax
from jax.experimental import pallas as pl
from jax.experimental.pallas import tpu as pltpu
from jax.sharding import Mesh, PartitionSpec as P

BLK = 128
AXES = ("zh", "x", "y", "z", "c")
SIZES = (2, 4, 4, 8, 2)
SECTION, FEAT = ("zh", "x"), ("y", "z", "c")
WIRE_Y = jnp.bfloat16
WIRE_Z = jnp.bfloat16


def swap_cores(block):
    return lax.ppermute(block, "c", [(0, 1), (1, 0)])


def exchange(block, axis):
    return lax.all_to_all(block, axis, split_axis=0, concat_axis=0, tiled=True)


def exchange_z(block):
    nz = SIZES[3]
    order = [list(range(i * nz, (i + 1) * nz))[:: -1 if i % 2 else 1] for i in range(SIZES[0])]
    return lax.all_to_all(
        block, ("zh", "z"), split_axis=0, concat_axis=0, axis_index_groups=order, tiled=True
    )


def gather(block, axis):
    copies = jnp.broadcast_to(block[None], (lax.axis_size(axis),) + block.shape)
    return exchange(copies, axis)


def with_neighbours(mine, beyond):
    layers, nz = SIZES[0] * SIZES[1], SIZES[3]
    even = lax.axis_index(SECTION) % 2 == 0
    rounds = []
    for first, sent in ((1, jnp.where(even, mine, beyond)), (0, jnp.where(even, beyond, mine))):
        route = []
        for i in range(first, layers - 1, 2):
            far = (i + 1) % SIZES[1] == 0
            for z in range(nz):
                here, there = i * nz + z, (i + 1) * nz + (nz - 1 - z if far else z)
                route += [(here, there), (there, here)]
        rounds.append(lax.ppermute(sent, SECTION + ("z",), route))
    upper, lower = rounds
    return jnp.where(even, upper, lower), jnp.where(even, lower, upper)


def column_blocks(error_ref, col):
    for z in range(error_ref.shape[1]):
        for r in range(error_ref.shape[3] // col):
            block = error_ref[:, z, :, r * col : (r + 1) * col]
            yield z, r, block.reshape(-1, col)


def grad_kernel(col, error_ref, *refs):
    *weight_refs, grad_ref, total = refs
    step = pl.program_id(0)
    feat_dev = weight_refs[0].shape[0]

    @pl.when(step == 0)
    def _():
        total[...] = jnp.zeros_like(total)

    for z, r, block in column_blocks(error_ref, col):
        for half in range(2):
            weight = weight_refs[2 * half + r][:, z * col : (z + 1) * col]
            total[:, half * feat_dev : (half + 1) * feat_dev] += lax.dot_general(
                block, weight, (((1,), (1,)), ((), ())), preferred_element_type=jnp.float32
            )

    @pl.when(step == pl.num_programs(0) - 1)
    def _():
        grad_ref[...] = total[...].astype(grad_ref.dtype)


def feature_grads(error, weights, weights_other):
    ny, nz, rows, both = error.shape
    feat_dev = weights.shape[0]
    steps = 4
    wide = weights.shape[1] // 2 // steps
    blocks = [
        pl.BlockSpec((feat_dev, wide), lambda j, r=r: (0, r * steps + j)) for r in range(2)
    ]
    return pl.pallas_call(
        functools.partial(grad_kernel, both // 2),
        grid=(steps,),
        in_specs=[pl.BlockSpec((ny, nz // steps, rows, both), lambda j: (0, j, 0, 0))] + 2 * blocks,
        out_specs=pl.BlockSpec((ny * rows, 2 * feat_dev), lambda j: (0, 0)),
        out_shape=jax.ShapeDtypeStruct((ny * rows, 2 * feat_dev), error.dtype),
        scratch_shapes=[pltpu.VMEM((ny * rows, 2 * feat_dev), jnp.float32)],
        compiler_params=pltpu.CompilerParams(vmem_limit_bytes=24 << 20),
        cost_estimate=pl.CostEstimate(
            flops=2 * error.size * 2 * feat_dev, bytes_accessed=5 << 20, transcendentals=0
        ),
    )(error, weights, weights, weights_other, weights_other)


def decoder_kernel(col, feature_ref, error_ref, other_ref, out_ref):
    half = feature_ref.shape[1] // 2
    for (z, r, block), (_, _, other) in zip(
        column_blocks(error_ref, col), column_blocks(other_ref, col)
    ):
        total = jnp.dot(feature_ref[:, :half], block, preferred_element_type=jnp.float32)
        total += jnp.dot(feature_ref[:, half:], other, preferred_element_type=jnp.float32)
        out_ref[r, :, z * col : (z + 1) * col] = total.astype(out_ref.dtype)


def decoder_grads(features, error, error_other):
    ny, nz, rows, both = error.shape
    feat_dev = features.shape[0]
    steps = 4
    block = pl.BlockSpec((ny, nz // steps, rows, both), lambda j: (0, j, 0, 0))
    width = nz * both // 2
    return pl.pallas_call(
        functools.partial(decoder_kernel, both // 2),
        grid=(steps,),
        in_specs=[pl.BlockSpec(features.shape, lambda j: (0, 0)), block, block],
        out_specs=pl.BlockSpec((2, feat_dev, width // steps), lambda j: (0, 0, j)),
        out_shape=jax.ShapeDtypeStruct((2, feat_dev, width), error.dtype),
        compiler_params=pltpu.CompilerParams(vmem_limit_bytes=24 << 20),
        cost_estimate=pl.CostEstimate(
            flops=4 * error.size * feat_dev, bytes_accessed=4 << 20, transcendentals=0
        ),
    )(features, error, error_other)


def per_device(pre_tiles, block_ids, thresholds, decoder, dec_bias, targets):
    bf16, f32 = jnp.bfloat16, jnp.float32
    ny, nz, nc = SIZES[2:]
    core = lax.axis_index("c")
    layer = lax.axis_index(SECTION)
    last_layer = SIZES[0] * SIZES[1] - 1
    tiles, ids = pre_tiles[0], block_ids[0]
    tok = tiles.shape[0]
    blocks = thresholds.shape[1] // BLK
    feat_dev = decoder.shape[1]
    width = decoder.shape[3]
    own_blocks = feat_dev // BLK
    col = width // nz

    order = jnp.arange(blocks, dtype=jnp.int32) ^ (core * own_blocks)
    selector = (ids[:, :, None] == order[None, None, :]).astype(bf16)
    dense = jnp.einsum("tkb,tkc->tbc", selector, tiles, preferred_element_type=f32)
    floor = thresholds[0].reshape(-1, nc, own_blocks, BLK)
    floor = jnp.where(core == 0, floor, floor[:, ::-1]).reshape(blocks, BLK)
    own = jnp.where(dense > floor[None], dense, 0.0).astype(bf16)
    sent = own.reshape(tok, ny * nz, nc * feat_dev).transpose(1, 0, 2)
    features = exchange(sent, ("y", "z")).reshape(ny * nz * tok, nc * feat_dev)
    f_mine, f_other = features[:, :feat_dev], features[:, feat_dev:]

    weights = lax.optimization_barrier(decoder[0].reshape(feat_dev, nc * width))
    weights_other = swap_cores(weights)
    weights_other = jnp.where(jnp.isnan(thresholds[0, 0]), jnp.zeros_like(weights), weights_other)

    part = jnp.dot(f_mine, weights, preferred_element_type=f32)
    part = part + jnp.dot(f_other, weights_other, preferred_element_type=f32)
    part = part.astype(WIRE_Y).reshape(ny, nz * tok, nc * width)
    part = jnp.sum(exchange(part, "y").astype(f32), axis=0)
    shift = dec_bias[0][None, :] - targets[0].astype(f32)
    shift = jnp.concatenate([shift, jnp.zeros_like(shift)], axis=1)
    here = jnp.arange(nz)[:, None, None] == lax.axis_index("z")
    part = part + jnp.where(here, shift[None], 0.0).reshape(part.shape)
    f_swapped = swap_cores(f_other)
    part, f_swapped = lax.optimization_barrier((part, f_swapped))
    part = part.reshape(nz * tok, nc, nz, col).transpose(2, 0, 1, 3).astype(WIRE_Z)
    part = part.reshape(nz, nz * tok, nc * col)
    part = jnp.sum(exchange_z(part).astype(f32), axis=0)

    mine, beyond = part[:, :col], part[:, col:]
    got, got_next = with_neighbours(mine, beyond)
    error_next = jnp.where(layer == last_layer, 0.0, beyond + got_next)
    error = jnp.concatenate([mine + got, error_next], axis=1).astype(bf16)

    error = exchange_z(jnp.broadcast_to(error[None], (nz,) + error.shape))
    error = gather(error, "y")
    error_other = swap_cores(error)

    grad = feature_grads(error, weights, weights_other).reshape(ny * nz, tok, -1)
    grad, error_other = lax.optimization_barrier((grad, error_other))
    returned = exchange(grad, ("y", "z"))

    f_own = jnp.concatenate([f_mine, f_swapped], axis=0).T
    grad_decoder = decoder_grads(f_own, error, error_other).transpose(1, 0, 2)[None]

    table = returned.transpose(1, 0, 2).reshape(tok, blocks, BLK)
    table = jnp.where(own > 0, table, jnp.zeros_like(table))
    picked = jnp.einsum("tkb,tbc->tkc", selector, table, preferred_element_type=f32)
    return picked.astype(bf16)[None], grad_decoder


def solution(mesh):
    split = Mesh(mesh.devices.reshape(SIZES), AXES)
    placed = (
        P(SECTION, FEAT, None, None),
        P(SECTION, FEAT, None),
        P(SECTION, None),
        P(SECTION, FEAT, None, None),
        P(SECTION, None),
        P(SECTION, FEAT, None),
    )
    return jax.shard_map(
        per_device,
        mesh=split,
        in_specs=placed,
        out_specs=(P(SECTION, FEAT, None, None), P(SECTION, FEAT, None, None)),
        check_vma=False,
    )
```

```python
import functools

import jax
import jax.numpy as jnp
from jax import lax
from jax.experimental import pallas as pl
from jax.experimental.pallas import tpu as pltpu
from jax.sharding import Mesh, PartitionSpec as P

BLK = 128
AXES = ("zh", "x", "y", "z", "c")
SIZES = (2, 4, 4, 8, 2)
SECTION, FEAT = ("zh", "x"), ("y", "z", "c")
WIRE_Y = jnp.bfloat16
WIRE_Z = jnp.bfloat16


def swap_cores(block):
    return lax.ppermute(block, "c", [(0, 1), (1, 0)])


def exchange(block, axis):
    return lax.all_to_all(block, axis, split_axis=0, concat_axis=0, tiled=True)


def exchange_z(block):
    nz = SIZES[3]
    order = [list(range(i * nz, (i + 1) * nz))[:: -1 if i % 2 else 1] for i in range(SIZES[0])]
    return lax.all_to_all(
        block, ("zh", "z"), split_axis=0, concat_axis=0, axis_index_groups=order, tiled=True
    )


def gather(block, axis):
    copies = jnp.broadcast_to(block[None], (lax.axis_size(axis),) + block.shape)
    return exchange(copies, axis)


def with_neighbours(mine, beyond):
    layers, nz = SIZES[0] * SIZES[1], SIZES[3]
    even = lax.axis_index(SECTION) % 2 == 0
    rounds = []
    for first, sent in ((1, jnp.where(even, mine, beyond)), (0, jnp.where(even, beyond, mine))):
        route = []
        for i in range(first, layers - 1, 2):
            far = (i + 1) % SIZES[1] == 0
            for z in range(nz):
                here, there = i * nz + z, (i + 1) * nz + (nz - 1 - z if far else z)
                route += [(here, there), (there, here)]
        rounds.append(lax.ppermute(sent, SECTION + ("z",), route))
    upper, lower = rounds
    return jnp.where(even, upper, lower), jnp.where(even, lower, upper)


def column_blocks(error_ref, col):
    for z in range(error_ref.shape[1]):
        for r in range(error_ref.shape[3] // col):
            block = error_ref[:, z, :, r * col : (r + 1) * col]
            yield z, r, block.reshape(-1, col)


def add_kernel(place_ref, part_ref, shift_ref, out_ref):
    pieces, rows, both = out_ref.shape
    col = both // 2
    tok = shift_ref.shape[0]
    own = lax.broadcasted_iota(jnp.int32, (rows, col), 0) - place_ref[0] * tok
    for z in range(pieces):
        for r in range(2):
            start = (r * pieces + z) * col
            total = part_ref[0, :, start : start + col].astype(jnp.float32)
            for y in range(1, part_ref.shape[0]):
                total += part_ref[y, :, start : start + col].astype(jnp.float32)
            if r == 0:
                for i in range(tok):
                    shift = shift_ref[i : i + 1, start : start + col]
                    total += jnp.where(own == i, shift, 0.0)
            out_ref[z, :, r * col : (r + 1) * col] = total.astype(out_ref.dtype)


def added(place, part, shift, pieces, dtype):
    _, rows, columns = part.shape
    return pl.pallas_call(
        add_kernel,
        in_specs=[
            pl.BlockSpec(memory_space=pltpu.SMEM),
            pl.BlockSpec(memory_space=pltpu.VMEM),
            pl.BlockSpec(memory_space=pltpu.VMEM),
        ],
        out_specs=pl.BlockSpec(memory_space=pltpu.VMEM),
        out_shape=jax.ShapeDtypeStruct((pieces, rows, columns // pieces), dtype),
        compiler_params=pltpu.CompilerParams(vmem_limit_bytes=16 << 20),
        cost_estimate=pl.CostEstimate(flops=part.size, bytes_accessed=2 << 20, transcendentals=0),
    )(place, part, shift)


def sum_kernel(feature_ref, mine_ref, other_ref, out_ref):
    feat_dev, columns = mine_ref.shape
    wide = 512
    for start in range(0, columns, wide):
        total = jnp.dot(
            feature_ref[:, :feat_dev],
            mine_ref[:, start : start + wide],
            preferred_element_type=jnp.float32,
        ) + jnp.dot(
            feature_ref[:, feat_dev:],
            other_ref[:, start : start + wide],
            preferred_element_type=jnp.float32,
        )
        out_ref[:, start : start + wide] = total.astype(out_ref.dtype)


def partial_sums(features, weights, weights_other, dtype):
    tokens = features.shape[0]
    return pl.pallas_call(
        sum_kernel,
        in_specs=[pl.BlockSpec(memory_space=pltpu.VMEM)] * 3,
        out_specs=pl.BlockSpec(memory_space=pltpu.VMEM),
        out_shape=jax.ShapeDtypeStruct((tokens, weights.shape[1]), dtype),
        compiler_params=pltpu.CompilerParams(vmem_limit_bytes=24 << 20),
        cost_estimate=pl.CostEstimate(
            flops=4 * tokens * weights.size, bytes_accessed=1 << 20, transcendentals=0
        ),
    )(features, weights, weights_other)


def grad_kernel(col, error_ref, mine_ref, other_ref, grad_ref, total):
    feat_dev = mine_ref.shape[0]
    pieces = error_ref.shape[1]
    for half, weight_ref in enumerate((mine_ref, other_ref)):
        place = slice(half * feat_dev, (half + 1) * feat_dev)
        for z, r, block in column_blocks(error_ref, col):
            start = (r * pieces + z) * col
            term = lax.dot_general(
                block,
                weight_ref[:, start : start + col],
                (((1,), (1,)), ((), ())),
                preferred_element_type=jnp.float32,
            )
            if z == 0 and r == 0:
                total[:, place] = term
            else:
                total[:, place] += term
    grad_ref[...] = total[...].astype(grad_ref.dtype)


def feature_grads(error, weights, weights_other):
    ny, nz, rows, both = error.shape
    feat_dev = weights.shape[0]
    return pl.pallas_call(
        functools.partial(grad_kernel, both // 2),
        in_specs=[pl.BlockSpec(memory_space=pltpu.VMEM)] * 3,
        out_specs=pl.BlockSpec(memory_space=pltpu.VMEM),
        out_shape=jax.ShapeDtypeStruct((ny * rows, 2 * feat_dev), error.dtype),
        scratch_shapes=[pltpu.VMEM((ny * rows, 2 * feat_dev), jnp.float32)],
        compiler_params=pltpu.CompilerParams(vmem_limit_bytes=24 << 20),
        cost_estimate=pl.CostEstimate(
            flops=2 * error.size * 2 * feat_dev, bytes_accessed=1 << 20, transcendentals=0
        ),
    )(error, weights, weights_other)


def decoder_kernel(col, feature_ref, error_ref, other_ref, out_ref):
    half = feature_ref.shape[1] // 2
    for (z, r, block), (_, _, other) in zip(
        column_blocks(error_ref, col), column_blocks(other_ref, col)
    ):
        total = jnp.dot(feature_ref[:, :half], block, preferred_element_type=jnp.float32)
        total += jnp.dot(feature_ref[:, half:], other, preferred_element_type=jnp.float32)
        out_ref[r, :, z * col : (z + 1) * col] = total.astype(out_ref.dtype)


def decoder_grads(features, error, error_other):
    ny, nz, rows, both = error.shape
    feat_dev = features.shape[0]
    steps = 4
    block = pl.BlockSpec((ny, nz // steps, rows, both), lambda j: (0, j, 0, 0))
    width = nz * both // 2
    return pl.pallas_call(
        functools.partial(decoder_kernel, both // 2),
        grid=(steps,),
        in_specs=[pl.BlockSpec(features.shape, lambda j: (0, 0)), block, block],
        out_specs=pl.BlockSpec((2, feat_dev, width // steps), lambda j: (0, 0, j)),
        out_shape=jax.ShapeDtypeStruct((2, feat_dev, width), error.dtype),
        compiler_params=pltpu.CompilerParams(vmem_limit_bytes=24 << 20),
        cost_estimate=pl.CostEstimate(
            flops=4 * error.size * feat_dev, bytes_accessed=4 << 20, transcendentals=0
        ),
    )(features, error, error_other)


def per_device(pre_tiles, block_ids, thresholds, decoder, dec_bias, targets):
    bf16, f32 = jnp.bfloat16, jnp.float32
    ny, nz, nc = SIZES[2:]
    core = lax.axis_index("c")
    layer = lax.axis_index(SECTION)
    last_layer = SIZES[0] * SIZES[1] - 1
    tiles, ids = pre_tiles[0], block_ids[0]
    tok = tiles.shape[0]
    blocks = thresholds.shape[1] // BLK
    feat_dev = decoder.shape[1]
    width = decoder.shape[3]
    own_blocks = feat_dev // BLK
    col = width // nz

    order = jnp.arange(blocks, dtype=jnp.int32) ^ (core * own_blocks)
    selector = (ids[:, :, None] == order[None, None, :]).astype(bf16)
    dense = jnp.einsum("tkb,tkc->tbc", selector, tiles, preferred_element_type=f32)
    floor = thresholds[0].reshape(-1, nc, own_blocks, BLK)
    floor = jnp.where(core == 0, floor, floor[:, ::-1]).reshape(blocks, BLK)
    own = jnp.where(dense > floor[None], dense, 0.0).astype(bf16)
    sent = own.reshape(tok, ny * nz, nc * feat_dev).transpose(1, 0, 2)
    features = exchange(sent, ("y", "z")).reshape(ny * nz * tok, nc * feat_dev)
    f_mine, f_other = features[:, :feat_dev], features[:, feat_dev:]

    weights = lax.optimization_barrier(decoder[0].reshape(feat_dev, nc * width))
    weights_other = swap_cores(weights)

    part = partial_sums(features, weights, weights_other, WIRE_Y)
    part = part.reshape(ny, nz * tok, nc * width)
    part = exchange(part, "y")
    shift = dec_bias[0][None, :] - targets[0].astype(f32)
    part = added(lax.axis_index("z")[None], part, shift, nz, WIRE_Z)
    f_swapped = swap_cores(f_other)
    part, f_swapped = lax.optimization_barrier((part, f_swapped))
    part = jnp.sum(exchange_z(part).astype(f32), axis=0)

    mine, beyond = part[:, :col], part[:, col:]
    got, got_next = with_neighbours(mine, beyond)
    error_next = jnp.where(layer == last_layer, 0.0, beyond + got_next)
    error = jnp.concatenate([mine + got, error_next], axis=1).astype(bf16)

    error = exchange_z(jnp.broadcast_to(error[None], (nz,) + error.shape))
    error = gather(error, "y")
    error_other = swap_cores(error)

    grad = feature_grads(error, weights, weights_other).reshape(ny * nz, tok, -1)
    grad, error_other = lax.optimization_barrier((grad, error_other))
    returned = exchange(grad, ("y", "z"))

    f_own = jnp.concatenate([f_mine, f_swapped], axis=0).T
    grad_decoder = decoder_grads(f_own, error, error_other).transpose(1, 0, 2)[None]

    table = returned.transpose(1, 0, 2).reshape(tok, blocks, BLK)
    table = jnp.where(own > 0, table, jnp.zeros_like(table))
    picked = jnp.einsum("tkb,tbc->tkc", selector, table, preferred_element_type=f32)
    return picked.astype(bf16)[None], grad_decoder


def solution(mesh):
    split = Mesh(mesh.devices.reshape(SIZES), AXES)
    placed = (
        P(SECTION, FEAT, None, None),
        P(SECTION, FEAT, None),
        P(SECTION, None),
        P(SECTION, FEAT, None, None),
        P(SECTION, None),
        P(SECTION, FEAT, None),
    )
    return jax.shard_map(
        per_device,
        mesh=split,
        in_specs=placed,
        out_specs=(P(SECTION, FEAT, None, None), P(SECTION, FEAT, None, None)),
        check_vma=False,
    )
```
